32 devices in a mesh: dp: 2 (over core), expert: 16 (over z, y, x).
Axes of the slice: x: 2, y: 2, z: 4, core: 2. Of those that a mesh axis runs over, the one named last changes fastest.
Arguments:
- tokens: bfloat16 [4096, 768], P(('dp', 'expert')), may hold values from -6 to 6
- cotangent: bfloat16 [4096, 768], P(('dp', 'expert')), may hold values from -6 to 6
- segment_ids: int32 [32, 128], P(('dp', 'expert')), may hold values from 0 to 7, never falling along the last dimension, each value on 1 to 32 neighbouring positions
- routes: int32 [4096, 1], P(('dp', 'expert')), may hold values from 0 to 7; in each aligned block of 128 rows (0 to 127, 128 to 255, ...) at most 32 rows name the same one
- bucket_table: int32 [257], replicated, may hold values from 0 to 31
- mixer_weight: bfloat16 [3072, 768], P(('dp', 'expert'))
- rel_bias: float32 [32, 12], replicated, may hold values from -4 to 4
- gain_attn: float32 [768], replicated, may hold values from 0.5 to 1.5
- gain_ffn: float32 [768], replicated, may hold values from 0.5 to 1.5
- router_weight: bfloat16 [768, 8], replicated, may hold values from -0.15625 to 0.15625
- expert_in: bfloat16 [16, 768, 1536], P('expert', 'dp'), may hold values from -0.21875 to 0.21875
- expert_out: bfloat16 [16, 768, 1536], P('expert', 'dp'), may hold values from -0.875 to 0.875
Outputs:
- mixed: bfloat16 [4096, 768], P(('dp', 'expert'))
- tokens_grad: float32 [4096, 768], P(('dp', 'expert'))
- mixer_grad: float32 [3072, 768], P(('dp', 'expert'))
- rel_bias_grad: float32 [32, 12], replicated
- gain_attn_grad: float32 [768], replicated
- gain_ffn_grad: float32 [768], replicated
- router_grad: float32 [768, 8], replicated
- expert_in_grad: float32 [16, 768, 1536], P('expert', 'dp')
- expert_out_grad: float32 [16, 768, 1536], P('expert', 'dp')
The draws below stay inside these ranges and needn't reach their ends.
Inputs may be any that keep to these rules, and one draw needn't show every extreme that they name: `routes`: in each sequence's 128 tokens, no expert is chosen more than 32 times; some expert is chosen exactly 32 times in some sequence. `segment_ids`: never falling along a sequence; a document has at most 32 tokens.
All inputs are finite; a program needn't handle non-finite values.
Results may differ from the reference program's by a relative error of at most 0.012.
The reference program's roundings to bfloat16 on the way count: a program that leaves them out, or rounds other values in their place, can miss the bound.
Values may be sent and summed in bfloat16 or wider, within the bound.
A program may use at most 128 MiB of HBM per device.

```python
import math
import jax
import jax.numpy as jnp
import numpy as np
from jax import lax

D = 768
HEADS = 12
HDIM = 64
FF = 3072
BUCKETS = 32
MAXDIST = 128
HALF = 1536
TOK_DEV = 128
EXPERTS = 8
CAP = 32
SEQS = 32
TOKENS = 4096


def draw_mixer_weight(key, part):
    key = jax.random.fold_in(key, 11)
    values = jax.random.normal(key, (4 * D, D), jnp.float32)
    rows = jnp.arange(4 * D)[:, None]
    scale = jnp.where(rows < 3 * D, 1.0, 4.0) / math.sqrt(D)
    return (values * scale).astype(jnp.bfloat16)


def with_ends(drawn, key, low, top_value):
    longest = drawn.shape.index(max(drawn.shape))
    spots = []
    for shift in (0, 1):
        where = [jax.random.randint(jax.random.fold_in(key, axis), (), 0, length) for axis, length in enumerate(drawn.shape)]
        where[longest] = (where[longest] + shift) % drawn.shape[longest]
        spots.append(tuple(where))
    return drawn.at[spots[0]].set(low).at[spots[1]].set(top_value)


def levels(own_key, extent, shards, low, top_value):
    def one(dim, blocks):
        steps = jax.random.uniform(jax.random.fold_in(jax.random.fold_in(own_key, 6), dim), (blocks,), jnp.float32, low / len(shards), top_value / len(shards))
        return jnp.repeat(jnp.exp(steps), extent[dim] // blocks).reshape((-1,) + (1,) * (len(extent) - dim - 1))

    level = one(*shards[0])
    for cut in shards[1:]:
        level = level * one(*cut)
    return level


def split_up(amount, total, most, skew):
    loads = [(1 << 20) // math.isqrt(rank ** skew) + 1 for rank in range(2, amount + 1)]
    surplus, given = total - most - (amount - 1), [1] * (amount - 1)
    while surplus > 0:
        movable = [i for i in range(amount - 1) if given[i] < most]
        pool, remaining = sum([loads[i] for i in movable]), surplus
        for i in movable:
            addition = min(most - given[i], max(1, remaining * loads[i] // pool), surplus)
            given[i] = given[i] + addition
            surplus = surplus - addition
    return np.array([most] + given)


def uneven_parts(own_key, amount, total, bound, skew):
    if amount == 2:
        one = jax.random.randint(own_key, (), max(1, total - bound), min(bound, total - 1) + 1)
        return jnp.stack([one, total - one])
    sizes = jnp.asarray(split_up(amount, total, bound, skew), jnp.int32)
    twos = (amount - 1) // 2
    giver, taker = sizes[1:1 + 2 * twos:2], sizes[2:2 + 2 * twos:2]
    margin = jnp.minimum(giver - 1, bound - taker)
    passed = jax.random.randint(jax.random.fold_in(own_key, 1), (twos,), 0, 1 << 20) % (margin + 1)
    sizes = sizes.at[1:1 + 2 * twos:2].set(giver - passed).at[2:2 + 2 * twos:2].set(taker + passed)
    return sizes[jax.random.permutation(jax.random.fold_in(own_key, 2), amount)]


def assign_block(key, own, number, rows, amount, top, most, skew):
    sequence = jax.random.permutation(key, amount)
    crowded, usual = shares(amount, rows * top, most, skew, True), shares(amount, rows * top, most, skew, False)
    places = jnp.arange(amount)

    def named(tallies, rotation):
        used = int((tallies > 0).sum())
        fixed = max(1, used // 4)
        moved = fixed + (places - fixed + rotation * (used - fixed)) % max(1, amount - fixed)
        return jnp.zeros((amount,), jnp.int32).at[sequence[jnp.where(places < fixed, places, moved)]].set(jnp.asarray(tallies, jnp.int32))

    tallies = jnp.where(number % 4 == 0, named(crowded, number // 4), named(usual, number - number // 4 - 1))
    mixed = jax.random.permutation(jax.random.fold_in(own, 3), amount)
    source_of, taker = mixed[0:amount // 2 * 2:2], mixed[1:amount // 2 * 2:2]
    slack = jnp.minimum(tallies[source_of] - 1, most - tallies[taker]) // 2
    slack = jnp.where((source_of == sequence[0]) | (taker == sequence[0]) | (tallies[taker] == 0), 0, jnp.maximum(slack, 0))
    moved = jax.random.randint(jax.random.fold_in(own, 4), (amount // 2,), 0, 1 << 20) % (slack + 1)
    tallies = tallies.at[source_of].add(-moved).at[taker].add(moved)
    labels = jnp.searchsorted(jnp.cumsum(tallies), jnp.arange(rows * top), side="right").astype(jnp.int32)
    table = labels.reshape(top, rows).T
    table = table[jax.random.permutation(jax.random.fold_in(own, 1), rows)]
    rotation = jax.random.randint(jax.random.fold_in(own, 2), (rows, 1), 0, top)
    return jnp.take_along_axis(table, (jnp.arange(top)[None, :] + rotation) % top, axis=1)


def shares(number_of, total, bound, skew, full):
    weights = [(1 << 20) // math.isqrt(rank ** skew) + 1 for rank in range(1, number_of + 1)]
    largest = bound if full else min(bound, max(-(-total // number_of), total * weights[0] // sum(weights)))
    least = 1 if total - largest >= number_of - 1 else 0
    holding, rest = [largest] + [least] * (number_of - 1), total - largest - least * (number_of - 1)
    while rest > 0:
        movable = [i for i in range(1, number_of) if holding[i] < largest] or [i for i in range(1, number_of) if holding[i] < bound]
        pool, remaining = sum([weights[i] for i in movable]), rest
        for i in movable:
            extra = min(bound - holding[i], max(1, remaining * weights[i] // pool), rest)
            holding[i] = holding[i] + extra
            rest = rest - extra
    return np.array(holding)


def noise(stream_key, shape, spread, limit, pieces=(), held_as=jnp.bfloat16):
    values = spread * jax.random.normal(stream_key, shape, jnp.float32)
    if pieces:
        values = values * levels(stream_key, shape, pieces, -0.22, 0.18)
    return jnp.clip(values, -limit, limit).astype(held_as)


def setup_inputs(seed: int = 0) -> dict:
    key_list = jax.random.split(jax.random.key(seed), 13)
    tokens = noise(key_list[0], (TOKENS, D), 1.0, 6.0, ((0, 32),))
    cotangent = noise(key_list[1], (TOKENS, D), 1.0, 6.0, ((0, 32),))
    segment_ids = jax.vmap(lambda own: jnp.searchsorted(jnp.cumsum(uneven_parts(own, 8, TOK_DEV, TOK_DEV // 4, 0)), jnp.arange(TOK_DEV), side="right"))(jax.random.split(key_list[2], SEQS)).reshape((SEQS, TOK_DEV)).astype(jnp.int32)
    routes_keys = jax.random.split(jax.random.fold_in(key_list[3], 1), TOKENS // TOK_DEV)
    routes_turns = jax.random.permutation(jax.random.fold_in(key_list[3], 3), TOKENS // TOK_DEV)
    routes = jax.vmap(lambda own, number: assign_block(jax.random.fold_in(key_list[3], 2), own, number, TOK_DEV, EXPERTS, 1, CAP, 2))(routes_keys, routes_turns).reshape((TOKENS, 1))
    bucket_table = with_ends(jax.random.randint(key_list[4], (2 * MAXDIST + 1,), 0, BUCKETS), jax.random.fold_in(key_list[4], 1), 0, BUCKETS - 1).astype(jnp.int32)
    mixer_weight = draw_mixer_weight(jax.random.fold_in(key_list[12], 71), 0)
    rel_bias = noise(key_list[6], (BUCKETS, HEADS), 1.0, 4.0, (), jnp.float32)
    gain_attn = jnp.clip(1.0 + 0.1 * jax.random.normal(key_list[7], (D,), jnp.float32), 0.5, 1.5)
    gain_ffn = jnp.clip(1.0 + 0.1 * jax.random.normal(key_list[8], (D,), jnp.float32), 0.5, 1.5)
    router_weight = noise(key_list[9], (D, EXPERTS), (2 * D) ** -0.5, 0.15625)
    expert_in = noise(key_list[10], (2 * EXPERTS, D, HALF), D ** -0.5, 0.21875, ((0, 16), (1, 2)))
    expert_out = noise(key_list[11], (2 * EXPERTS, D, HALF), (max(1, FF // (EXPERTS * EXPERTS))) ** -0.5, 0.875, ((0, 16), (1, 2)))
    return {"tokens": tokens, "cotangent": cotangent, "segment_ids": segment_ids, "routes": routes, "bucket_table": bucket_table, "mixer_weight": mixer_weight, "rel_bias": rel_bias, "gain_attn": gain_attn, "gain_ffn": gain_ffn, "router_weight": router_weight, "expert_in": expert_in, "expert_out": expert_out}


@jax.custom_vjp
def low(v):
    return lax.optimization_barrier(v.astype(jnp.bfloat16)).astype(jnp.float32)

@jax.custom_vjp
def low_back(v):
    return v

def low_keep(v):
    return (low(v), None)

def low_pass(kept, grad):
    return (grad,)

def back_keep(v):
    return (v, None)

def back_low(kept, grad):
    return (low(grad),)
low.defvjp(low_keep, low_pass)
low_back.defvjp(back_keep, back_low)

def rms_scale(rows, gain):
    inverse = lax.rsqrt(lax.optimization_barrier(jnp.mean(rows * rows, axis=-1, keepdims=True)) + 1e-06)
    return rows * inverse * gain

def reference(tokens, cotangent, segment_ids, routes, bucket_table, mixer_weight, rel_bias, gain_attn, gain_ffn, router_weight, expert_in, expert_out):
    f32 = jnp.float32
    highest = lax.Precision.HIGHEST
    route = routes[:, 0].astype(jnp.int32)
    chosen = (route[:, None] == jnp.arange(EXPERTS, dtype=jnp.int32)[None, :]).astype(f32)
    order = jnp.argsort(route, stable=True).astype(jnp.int32)
    counts = lax.optimization_barrier(jnp.sum(chosen, axis=0)).astype(jnp.int32)
    starts = (jnp.cumsum(counts) - counts).astype(jnp.int32)
    lanes = jnp.arange(SEQS * CAP, dtype=jnp.int32)
    positions = jnp.clip(starts[:, None] + lanes[None, :], 0, TOKENS - 1).astype(jnp.int32)
    picked = jnp.where(lanes[None, :] < counts[:, None], order[positions], TOKENS).astype(jnp.int32)
    spacing = jnp.arange(TOK_DEV, dtype=jnp.int32)[None, :] - jnp.arange(TOK_DEV, dtype=jnp.int32)[:, None]
    bucket = bucket_table[(jnp.clip(spacing, -MAXDIST, MAXDIST) + MAXDIST).astype(jnp.int32)]
    bucket_hot = (bucket[:, :, None] == jnp.arange(BUCKETS, dtype=jnp.int32)[None, None, :]).astype(f32)

    def forward(xf, mixer, bias_table, gain_one, gain_two, router, inner, outer):
        n1 = low(rms_scale(xf, gain_one))
        qkv = low_back(low(jnp.dot(n1, mixer[:3 * D].T, precision=highest)))
        bias = jnp.einsum('ijb,bh->hij', bucket_hot, bias_table, precision=highest)

        def one_sequence(block):
            queries, keys, values, segment = block
            queries = queries.reshape(TOK_DEV, HEADS, HDIM)
            keys = keys.reshape(TOK_DEV, HEADS, HDIM)
            values = values.reshape(TOK_DEV, HEADS, HDIM)
            product = low_back(jnp.einsum('ihd,jhd->hij', queries, keys, precision=highest))
            scores = product * HDIM ** (-0.5) + bias
            same = (segment[:, None] == segment[None, :])[None]
            scores = jnp.where(same, scores, -1e+30)
            probs = jax.nn.softmax(scores, axis=-1)
            return jnp.einsum('hij,jhd->ihd', low(probs), values, precision=highest).reshape(TOK_DEV, D)
        attended = lax.map(jax.checkpoint(one_sequence), (qkv[:, :D].reshape(SEQS, TOK_DEV, D), qkv[:, D:2 * D].reshape(SEQS, TOK_DEV, D), qkv[:, 2 * D:].reshape(SEQS, TOK_DEV, D), segment_ids))
        attended = low_back(low(attended.reshape(TOKENS, D)))
        x_mid = xf + low_back(jnp.dot(attended, mixer[3 * D:].T, precision=highest))
        n2 = low(rms_scale(x_mid, gain_two))
        logits = low_back(jnp.dot(n2, router, precision=highest))
        gate = lax.optimization_barrier(jnp.sum(jax.nn.softmax(logits, axis=-1) * chosen, axis=-1))
        full_in = inner.reshape(EXPERTS, 2, D, HALF).transpose(0, 2, 1, 3).reshape(EXPERTS, D, FF)
        full_out = outer.reshape(EXPERTS, 2, D, HALF).transpose(0, 2, 1, 3).reshape(EXPERTS, D, FF)
        padded = jnp.concatenate([n2, jnp.zeros((1, D), f32)], axis=0)
        gathered = padded[picked]

        def one_expert(block):
            rows, w_first, w_second = block
            hidden = low_back(jnp.dot(rows, w_first, precision=highest))
            active = low(jax.nn.gelu(hidden, approximate=True))
            return jnp.dot(active, w_second.T, precision=highest)
        results = lax.map(jax.checkpoint(one_expert), (gathered, full_in, full_out))
        summed = jnp.zeros((TOKENS + 1, D), f32).at[picked.reshape(-1)].add(results.reshape(-1, D))[:TOKENS]
        summed = low_back(summed)
        return x_mid + gate[:, None] * summed
    primals = (tokens.astype(f32), mixer_weight.astype(f32), rel_bias.astype(f32), gain_attn.astype(f32), gain_ffn.astype(f32), router_weight.astype(f32), expert_in.astype(f32), expert_out.astype(f32))
    output, pullback = jax.vjp(forward, *primals)
    grads = pullback(cotangent.astype(f32))
    return (output.astype(jnp.bfloat16), grads[0], grads[1], grads[2], grads[3], grads[4], grads[5], grads[6], grads[7])
```

```python
import jax
import jax.numpy as jnp
from jax import lax
from jax.sharding import PartitionSpec as P


def rms_scale(rows, gain):
    inverse = lax.rsqrt(jnp.mean(rows * rows, axis=-1, keepdims=True) + 1e-06)
    return rows * inverse * gain


def gate_value(logits, chosen):
    return jnp.sum(jax.nn.softmax(logits, axis=-1) * chosen, axis=-1)


def tanh_gelu(values):
    return jax.nn.gelu(values, approximate=True)


def contract_first(left, right):
    return lax.dot_general(
        left, right, (((0,), (0,)), ((), ())), preferred_element_type=jnp.float32
    )


def contract_last(left, right):
    return lax.dot_general(
        left, right, (((1,), (1,)), ((), ())), preferred_element_type=jnp.float32
    )


def skewed_table(table, count, reach):
    offsets = jnp.arange(2 * count)
    offsets = jnp.where(offsets < count, offsets, offsets - 2 * count)
    index = jnp.clip(offsets, -reach, reach) + reach
    hot = index[:, None] == jnp.arange(table.shape[0])[None, :]
    line = jnp.sum(jnp.where(hot, table[None, :], 0), axis=1)
    flat = jnp.broadcast_to(line[None, :], (count, 2 * count)).reshape(-1)
    return flat[: count * (2 * count - 1)].reshape(count, 2 * count - 1)[:, :count]


def deliver(buffer, experts, capacity, width):
    doubled = jnp.broadcast_to(
        buffer.reshape(experts, 1, capacity, width), (experts, 2, capacity, width)
    )
    return lax.all_to_all(
        doubled.reshape(2 * experts * capacity, width),
        "expert",
        split_axis=0,
        concat_axis=0,
        tiled=True,
    )


def collect(results, experts, capacity, width):
    returned = lax.all_to_all(results, "expert", split_axis=0, concat_axis=0, tiled=True)
    returned = returned.reshape(experts, 2, capacity, width)
    return [returned[:, half].reshape(experts * capacity, width) for half in (0, 1)]


def shards(
    tokens,
    cotangent,
    segment_ids,
    routes,
    bucket_table,
    mixer_weight,
    rel_bias,
    gain_attn,
    gain_ffn,
    router_weight,
    expert_in,
    expert_out,
):
    f32 = jnp.float32
    bf16 = jnp.bfloat16
    highest = lax.Precision.HIGHEST
    count, width = tokens.shape
    buckets, heads = rel_bias.shape
    head_dim = width // heads
    experts = router_weight.shape[1]
    capacity = 2 * max(1, count // experts)
    reach = (bucket_table.shape[0] - 1) // 2
    scale = head_dim ** (-0.5)
    mixer = lax.all_gather(mixer_weight, ("dp", "expert"), axis=0, tiled=True)
    inner_all, outer_all = (
        lax.all_gather(expert_in, "dp", axis=1, tiled=True),
        lax.all_gather(expert_out, "dp", axis=1, tiled=True),
    )
    w_inner = inner_all[0]
    w_outer = outer_all[0]
    xf = tokens.astype(f32)
    norm_one, norm_one_back = jax.vjp(rms_scale, xf, gain_attn)
    normed_one = norm_one.astype(bf16)
    qkv = contract_last(normed_one, mixer[: 3 * width]).astype(bf16)
    queries = qkv[:, :width].reshape(count, heads, head_dim)
    keys = qkv[:, width : 2 * width].reshape(count, heads, head_dim)
    values = qkv[:, 2 * width :].reshape(count, heads, head_dim)
    bucket = skewed_table(bucket_table, count, reach)
    bucket_hot = (bucket[:, :, None] == jnp.arange(buckets)[None, None, :]).astype(f32)
    bias = jnp.einsum("ijb,bh->hij", bucket_hot, rel_bias, precision=highest)
    segment = segment_ids[0]
    same = (segment[:, None] == segment[None, :])[None]
    scores = jnp.einsum("ihd,jhd->hij", queries, keys, preferred_element_type=f32) * scale + bias
    scores = jnp.where(same, scores, -1e30)
    peak = jnp.max(scores, axis=-1, keepdims=True)
    weights = jnp.exp(scores - peak)
    probs = weights / jnp.sum(weights, axis=-1, keepdims=True)
    probs_low = probs.astype(bf16)
    attended = (
        jnp.einsum("hij,jhd->ihd", probs_low, values, preferred_element_type=f32)
        .astype(bf16)
        .reshape(count, width)
    )
    x_mid = xf + contract_last(attended, mixer[3 * width :])
    norm_two, norm_two_back = jax.vjp(rms_scale, x_mid, gain_ffn)
    normed_two = norm_two.astype(bf16)
    logits = jnp.dot(normed_two, router_weight, preferred_element_type=f32)
    route = routes[:, 0]
    chosen = (route[:, None] == jnp.arange(experts)[None, :]).astype(f32)
    gate, gate_back = jax.vjp(lambda scores_in: gate_value(scores_in, chosen), logits)
    below = (jnp.arange(count)[:, None] > jnp.arange(count)[None, :]).astype(bf16)
    earlier = jnp.dot(below, chosen.astype(bf16), preferred_element_type=f32)
    slot = jnp.sum(earlier * chosen, axis=1).astype(jnp.int32)
    column = route * capacity + slot
    place_hot = column[:, None] == jnp.arange(experts * capacity)[None, :]
    place = place_hot.astype(bf16)
    upstream = cotangent.astype(f32)
    expert_grad_tok = (gate[:, None] * upstream).astype(bf16)
    both = jnp.concatenate([normed_two, expert_grad_tok], axis=1)
    buffer = contract_first(place, both).astype(bf16)
    arrived_both = deliver(buffer, experts, capacity, 2 * width)
    arrived, grad_arrived = arrived_both[:, :width], arrived_both[:, width:]
    hidden = jnp.dot(arrived, w_inner, preferred_element_type=f32)
    active, active_back = jax.vjp(tanh_gelu, hidden)
    active_low = active.astype(bf16)
    partial_rows = contract_last(active_low, w_outer).astype(bf16)
    active_grad = jnp.dot(grad_arrived, w_outer, preferred_element_type=f32)
    hidden_grad = active_back(active_grad)[0].astype(bf16)
    input_part = contract_last(hidden_grad, w_inner).astype(bf16)
    outer_grad = contract_first(grad_arrived, active_low)
    inner_grad = contract_first(arrived, hidden_grad)
    inner_share, outer_share = (
        lax.psum_scatter(inner_grad[None], "dp", scatter_dimension=1, tiled=True),
        lax.psum_scatter(outer_grad[None], "dp", scatter_dimension=1, tiled=True),
    )
    results = collect(
        jnp.concatenate([partial_rows, input_part], axis=1), experts, capacity, 2 * width
    )
    tok_both = jnp.dot(place, results[0], preferred_element_type=f32) + jnp.dot(
        place, results[1], preferred_element_type=f32
    )
    expert_tok, input_tok = tok_both[:, :width], tok_both[:, width:]
    mixed = (x_mid + gate[:, None] * expert_tok).astype(bf16)
    gate_grad = jnp.sum(upstream * expert_tok, axis=1)
    logit_grad = gate_back(gate_grad)[0].astype(bf16)
    router_local = contract_first(normed_two, logit_grad)
    norm_two_grad = input_tok + contract_last(logit_grad, router_weight)
    mid_part, gain_ffn_local = norm_two_back(norm_two_grad)
    mid_grad = upstream + mid_part
    branch_grad = mid_grad.astype(bf16)
    out_block_grad = contract_first(branch_grad, attended)
    attended_grad = (
        jnp.dot(branch_grad, mixer[3 * width :], preferred_element_type=f32)
        .astype(bf16)
        .reshape(count, heads, head_dim)
    )
    prob_grad = jnp.einsum("ihd,jhd->hij", attended_grad, values, preferred_element_type=f32)
    score_grad = probs * (prob_grad - jnp.sum(prob_grad * probs, axis=-1, keepdims=True))
    bias_local = jnp.einsum("hij,ijb->bh", score_grad, bucket_hot, precision=highest)
    product_grad = (score_grad * scale).astype(bf16)
    query_grad = jnp.einsum("hij,jhd->ihd", product_grad, keys, preferred_element_type=f32).astype(
        bf16
    )
    key_grad = jnp.einsum("hij,ihd->jhd", product_grad, queries, preferred_element_type=f32).astype(
        bf16
    )
    value_grad = jnp.einsum(
        "hij,ihd->jhd", probs_low, attended_grad, preferred_element_type=f32
    ).astype(bf16)
    qkv_grad = jnp.concatenate(
        [
            query_grad.reshape(count, width),
            key_grad.reshape(count, width),
            value_grad.reshape(count, width),
        ],
        axis=1,
    )
    in_block_grad = contract_first(qkv_grad, normed_one)
    norm_one_grad = jnp.dot(qkv_grad, mixer[: 3 * width], preferred_element_type=f32)
    input_part_one, gain_attn_local = norm_one_back(norm_one_grad)
    tokens_grad = mid_grad + input_part_one
    mixer_grad = lax.psum_scatter(
        jnp.concatenate([in_block_grad, out_block_grad], axis=0).astype(bf16),
        ("dp", "expert"),
        scatter_dimension=0,
        tiled=True,
    ).astype(f32)
    pieces = (bias_local, gain_attn_local, gain_ffn_local, router_local)
    flat = jnp.concatenate([piece.reshape(-1) for piece in pieces])
    total = lax.psum(flat.reshape(-1, 128), ("dp", "expert")).reshape(-1)
    sums, start = [], 0
    for piece in pieces:
        sums.append(total[start : start + piece.size].reshape(piece.shape))
        start += piece.size
    bias_sum, attn_gain_sum, ffn_gain_sum, router_sum = sums
    return (
        mixed,
        tokens_grad,
        mixer_grad,
        bias_sum,
        attn_gain_sum,
        ffn_gain_sum,
        router_sum,
        inner_share,
        outer_share,
    )


def solution(mesh):
    placed = (
        P(("dp", "expert"), None),
        P(("dp", "expert"), None),
        P(("dp", "expert"), None),
        P(("dp", "expert"), None),
        P(),
        P(("dp", "expert"), None),
        P(),
        P(),
        P(),
        P(),
        P("expert", "dp", None),
        P("expert", "dp", None),
    )
    return jax.shard_map(
        shards,
        mesh=mesh,
        in_specs=placed,
        out_specs=(
            P(("dp", "expert"), None),
            P(("dp", "expert"), None),
            P(("dp", "expert"), None),
            P(),
            P(),
            P(),
            P(),
            P("expert", "dp", None),
            P("expert", "dp", None),
        ),
        check_vma=False,
    )
```

```python
import jax
import jax.numpy as jnp
from jax import lax
from jax.experimental import pallas as pl
from jax.experimental.pallas import tpu as pltpu
from jax.sharding import PartitionSpec as P


def rms_scale(rows, gain):
    inverse = lax.rsqrt(jnp.mean(rows * rows, axis=-1, keepdims=True) + 1e-06)
    return rows * inverse * gain


def gate_value(logits, chosen):
    return jnp.sum(jax.nn.softmax(logits, axis=-1) * chosen, axis=-1)


def tanh_gelu(values):
    return jax.nn.gelu(values, approximate=True)


def contract_first(left, right):
    return lax.dot_general(
        left, right, (((0,), (0,)), ((), ())), preferred_element_type=jnp.float32
    )


def contract_last(left, right):
    return lax.dot_general(
        left, right, (((1,), (1,)), ((), ())), preferred_element_type=jnp.float32
    )


def skewed_table(table, count, reach):
    offsets = jnp.arange(2 * count)
    offsets = jnp.where(offsets < count, offsets, offsets - 2 * count)
    index = jnp.clip(offsets, -reach, reach) + reach
    hot = index[:, None] == jnp.arange(table.shape[0])[None, :]
    line = jnp.sum(jnp.where(hot, table[None, :], 0), axis=1)
    flat = jnp.broadcast_to(line[None, :], (count, 2 * count)).reshape(-1)
    return flat[: count * (2 * count - 1)].reshape(count, 2 * count - 1)[:, :count]


def deliver(buffer, experts, capacity, width):
    doubled = jnp.broadcast_to(
        buffer.reshape(experts, 1, capacity, width), (experts, 2, capacity, width)
    )
    return lax.all_to_all(
        doubled.reshape(2 * experts * capacity, width),
        "expert",
        split_axis=0,
        concat_axis=0,
        tiled=True,
    )


def collect(results, experts, capacity, width):
    returned = lax.all_to_all(results, "expert", split_axis=0, concat_axis=0, tiled=True)
    returned = returned.reshape(experts, 2, capacity, width)
    return [returned[:, half].reshape(experts * capacity, width) for half in (0, 1)]


MESH = pl.DeviceIdType.MESH


def coordinates():
    core, chip = lax.axis_index("dp"), lax.axis_index("expert")
    bits = [chip // 8, (chip // 4) % 2, (chip // 2) % 2, chip % 2]
    partners = [(core, chip + (1 - 2 * bit) * step) for bit, step in zip(bits, (8, 4, 2, 1))]
    return core, bits, (1 - core, chip), partners


def meet(partners):
    barrier = pltpu.get_barrier_semaphore()
    for partner in partners:
        pl.semaphore_signal(barrier, inc=1, device_id=partner, device_id_type=MESH)
    pl.semaphore_wait(barrier, len(partners))


def gather_kernel(own_ref, out_ref, local_sem, send_sem, recv_sem):
    core, (high, low, y, x), sibling, (to_high, to_low, to_y, to_x) = coordinates()
    half = own_ref.shape[1] // 2
    left, right = pl.ds(0, half), pl.ds(half, half)
    every = slice(None)
    local = pltpu.make_async_copy(own_ref, out_ref.at[core, high, low, y, x], local_sem)
    local.start()
    meet((sibling, to_high, to_low, to_y, to_x))
    local.wait()

    def send(number, where, target):
        copy = pltpu.make_async_remote_copy(
            src_ref=out_ref.at[where],
            dst_ref=out_ref.at[where],
            send_sem=send_sem.at[number],
            recv_sem=recv_sem.at[number],
            device_id=target,
            device_id_type=MESH,
        )
        copy.start()
        return copy

    first = send(0, (core, high, low, y, x), to_high)
    first.wait_recv()
    second = send(1, (core, every, low, y, x), to_low)
    second.wait_recv()
    third_a = send(2, (core, every, every, y, x, every, left), to_y)
    third_b = send(3, (core, every, every, y, x, every, right), to_x)
    across = [send(6, (core, every, every, y, x), sibling)]
    third_a.wait_recv()
    fourth_a = send(4, (core, every, every, every, x, every, left), to_x)
    third_b.wait_recv()
    fourth_b = send(5, (core, every, every, y, every, every, right), to_y)
    across.append(send(7, (core, every, every, 1 - y, x, every, left), sibling))
    across.append(send(8, (core, every, every, y, 1 - x, every, right), sibling))
    fourth_a.wait_recv()
    across.append(send(9, (core, every, every, every, 1 - x, every, left), sibling))
    fourth_b.wait_recv()
    across.append(send(10, (core, every, every, 1 - y, every, every, right), sibling))
    for copy in across:
        copy.wait_recv()
    for copy in [first, second, third_a, third_b, fourth_a, fourth_b] + across:
        copy.wait_send()


def gather_mixer(block):
    rows, width = block.shape
    out = pl.pallas_call(
        gather_kernel,
        out_shape=jax.ShapeDtypeStruct((2, 2, 2, 2, 2, rows, width), block.dtype),
        in_specs=[pl.BlockSpec(memory_space=pl.ANY)],
        out_specs=pl.BlockSpec(memory_space=pl.ANY),
        scratch_shapes=[
            pltpu.SemaphoreType.DMA,
            pltpu.SemaphoreType.DMA((11,)),
            pltpu.SemaphoreType.DMA((11,)),
        ],
        compiler_params=pltpu.CompilerParams(collective_id=0, has_side_effects=True),
    )(block)
    return out.reshape(32 * rows, width)


def scatter_kernel(
    grad_ref,
    small_ref,
    out_ref,
    total_ref,
    whole,
    pair,
    quad,
    line,
    from_core,
    from_a,
    from_b,
    then_a,
    then_b,
    from_low,
    from_high,
    sums,
    arrived,
    send_sem,
    recv_sem,
):
    core, (high, low, y, x), sibling, (to_high, to_low, to_y, to_x) = coordinates()
    f32, bf16 = jnp.float32, jnp.bfloat16
    half = out_ref.shape[1] // 2
    left, right = pl.ds(0, half), pl.ds(half, half)
    every = slice(None)
    meet((sibling, to_high, to_low, to_y, to_x))

    def send(number, source, target_ref, target):
        copy = pltpu.make_async_remote_copy(
            src_ref=source,
            dst_ref=target_ref,
            send_sem=send_sem.at[number],
            recv_sem=recv_sem.at[number],
            device_id=target,
            device_id_type=MESH,
        )
        copy.start()
        return copy

    started = []
    order = (sibling, to_x, to_y, to_low, to_high)

    def small_start(stage):
        copy = send(7 + stage, sums.at[stage], arrived.at[stage], order[stage])
        started.append(copy)
        return copy

    def small_end(stage, copy):
        copy.wait_recv()
        sums[stage + 1] = sums[stage] + arrived[stage]

    def add(one, two):
        return one.astype(f32) + two.astype(f32)

    sums[0] = small_ref[...]
    copy = send(0, grad_ref.at[1 - core], from_core, sibling)
    small = small_start(0)
    copy.wait_recv()
    started.append(copy)
    for a in (0, 1):
        for b in (0, 1):
            for c in (0, 1):
                for d in (0, 1):
                    whole[a, b, c, d] = add(
                        grad_ref[core, a, b, c, d], from_core[a, b, c, d]
                    ).astype(bf16)
    one = send(1, whole.at[:, :, :, 1 - x, :, left], from_a, to_x)
    two = send(2, whole.at[:, :, 1 - y, :, :, right], from_b, to_y)
    started += [one, two]
    small_end(0, small)
    small = small_start(1)
    one.wait_recv()
    for a in (0, 1):
        for b in (0, 1):
            for c in (0, 1):
                pair[0, a, b, c] = add(whole[a, b, c, x, :, :half], from_a[a, b, c]).astype(bf16)
    three = send(3, pair.at[0, :, :, 1 - y], then_a, to_y)
    two.wait_recv()
    for a in (0, 1):
        for b in (0, 1):
            for c in (0, 1):
                pair[1, a, b, c] = add(whole[a, b, y, c, :, half:], from_b[a, b, c]).astype(bf16)
    four = send(4, pair.at[1, :, :, 1 - x], then_b, to_x)
    started += [three, four]
    small_end(1, small)
    small = small_start(2)
    three.wait_recv()
    four.wait_recv()
    for a in (0, 1):
        for b in (0, 1):
            quad[a, b, :, :half] = add(pair[0, a, b, y], then_a[a, b]).astype(bf16)
            quad[a, b, :, half:] = add(pair[1, a, b, x], then_b[a, b]).astype(bf16)
    five = send(5, quad.at[:, 1 - low], from_low, to_low)
    started.append(five)
    small_end(2, small)
    small = small_start(3)
    five.wait_recv()
    for a in (0, 1):
        line[a] = add(quad[a, low], from_low[a]).astype(bf16)
    six = send(6, line.at[1 - high], from_high, to_high)
    started.append(six)
    small_end(3, small)
    small = small_start(4)
    six.wait_recv()
    out_ref[...] = add(line[high], from_high[...])
    small.wait_recv()
    total_ref[...] = sums[4] + arrived[4]
    for copy in started:
        copy.wait_send()


def scatter_mixer(grad, small):
    rows, width = grad.shape[0] // 32, grad.shape[1]
    bf16, f32 = grad.dtype, jnp.float32
    half = width // 2
    vmem = pl.BlockSpec(memory_space=pltpu.VMEM)
    return pl.pallas_call(
        scatter_kernel,
        out_shape=(
            jax.ShapeDtypeStruct((rows, width), f32),
            jax.ShapeDtypeStruct(small.shape, f32),
        ),
        in_specs=[vmem, vmem],
        out_specs=(vmem, vmem),
        scratch_shapes=[
            pltpu.VMEM((2, 2, 2, 2, rows, width), bf16),
            pltpu.VMEM((2, 2, 2, 2, rows, half), bf16),
            pltpu.VMEM((2, 2, rows, width), bf16),
            pltpu.VMEM((2, rows, width), bf16),
            pltpu.VMEM((2, 2, 2, 2, rows, width), bf16),
            pltpu.VMEM((2, 2, 2, rows, half), bf16),
            pltpu.VMEM((2, 2, 2, rows, half), bf16),
            pltpu.VMEM((2, 2, rows, half), bf16),
            pltpu.VMEM((2, 2, rows, half), bf16),
            pltpu.VMEM((2, rows, width), bf16),
            pltpu.VMEM((rows, width), bf16),
            pltpu.VMEM((5,) + small.shape, f32),
            pltpu.VMEM((5,) + small.shape, f32),
            pltpu.SemaphoreType.DMA((12,)),
            pltpu.SemaphoreType.DMA((12,)),
        ],
        compiler_params=pltpu.CompilerParams(
            collective_id=1, has_side_effects=True, vmem_limit_bytes=40 * 2**20
        ),
        cost_estimate=pl.CostEstimate(
            flops=0, bytes_accessed=120 * 2**20, transcendentals=0
        ),
    )(grad.reshape(2, 2, 2, 2, 2, rows, width), small)


def shards(
    tokens,
    cotangent,
    segment_ids,
    routes,
    bucket_table,
    mixer_weight,
    rel_bias,
    gain_attn,
    gain_ffn,
    router_weight,
    expert_in,
    expert_out,
):
    f32 = jnp.float32
    bf16 = jnp.bfloat16
    highest = lax.Precision.HIGHEST
    count, width = tokens.shape
    buckets, heads = rel_bias.shape
    head_dim = width // heads
    experts = router_weight.shape[1]
    capacity = 2 * max(1, count // experts)
    reach = (bucket_table.shape[0] - 1) // 2
    scale = head_dim ** (-0.5)
    cube = (
        lax.axis_size("dp") == 2
        and lax.axis_size("expert") == 16
        and mixer_weight.shape[0] % 16 == 0
        and width % 256 == 0
    )
    if cube:
        mixer = gather_mixer(mixer_weight)
    else:
        mixer = lax.all_gather(mixer_weight, ("dp", "expert"), axis=0, tiled=True)
    inner_all, outer_all = (
        lax.all_gather(expert_in, "dp", axis=1, tiled=True),
        lax.all_gather(expert_out, "dp", axis=1, tiled=True),
    )
    w_inner = inner_all[0]
    w_outer = outer_all[0]
    xf = tokens.astype(f32)
    norm_one, norm_one_back = jax.vjp(rms_scale, xf, gain_attn)
    normed_one = norm_one.astype(bf16)
    qkv = contract_last(normed_one, mixer[: 3 * width]).astype(bf16)
    queries = qkv[:, :width].reshape(count, heads, head_dim)
    keys = qkv[:, width : 2 * width].reshape(count, heads, head_dim)
    values = qkv[:, 2 * width :].reshape(count, heads, head_dim)
    bucket = skewed_table(bucket_table, count, reach)
    bucket_hot = (bucket[:, :, None] == jnp.arange(buckets)[None, None, :]).astype(f32)
    bias = jnp.einsum("ijb,bh->hij", bucket_hot, rel_bias, precision=highest)
    segment = segment_ids[0]
    same = (segment[:, None] == segment[None, :])[None]
    scores = jnp.einsum("ihd,jhd->hij", queries, keys, preferred_element_type=f32) * scale + bias
    scores = jnp.where(same, scores, -1e30)
    peak = jnp.max(scores, axis=-1, keepdims=True)
    weights = jnp.exp(scores - peak)
    probs = weights / jnp.sum(weights, axis=-1, keepdims=True)
    probs_low = probs.astype(bf16)
    attended = (
        jnp.einsum("hij,jhd->ihd", probs_low, values, preferred_element_type=f32)
        .astype(bf16)
        .reshape(count, width)
    )
    x_mid = xf + contract_last(attended, mixer[3 * width :])
    norm_two, norm_two_back = jax.vjp(rms_scale, x_mid, gain_ffn)
    normed_two = norm_two.astype(bf16)
    logits = jnp.dot(normed_two, router_weight, preferred_element_type=f32)
    route = routes[:, 0]
    chosen = (route[:, None] == jnp.arange(experts)[None, :]).astype(f32)
    gate, gate_back = jax.vjp(lambda scores_in: gate_value(scores_in, chosen), logits)
    below = (jnp.arange(count)[:, None] > jnp.arange(count)[None, :]).astype(bf16)
    earlier = jnp.dot(below, chosen.astype(bf16), preferred_element_type=f32)
    slot = jnp.sum(earlier * chosen, axis=1).astype(jnp.int32)
    column = route * capacity + slot
    place_hot = column[:, None] == jnp.arange(experts * capacity)[None, :]
    place = place_hot.astype(bf16)
    upstream = cotangent.astype(f32)
    expert_grad_tok = (gate[:, None] * upstream).astype(bf16)
    both = jnp.concatenate([normed_two, expert_grad_tok], axis=1)
    buffer = contract_first(place, both).astype(bf16)
    arrived_both = deliver(buffer, experts, capacity, 2 * width)
    arrived, grad_arrived = arrived_both[:, :width], arrived_both[:, width:]
    hidden = jnp.dot(arrived, w_inner, preferred_element_type=f32)
    active, active_back = jax.vjp(tanh_gelu, hidden)
    active_low = active.astype(bf16)
    partial_rows = contract_last(active_low, w_outer).astype(bf16)
    active_grad = jnp.dot(grad_arrived, w_outer, preferred_element_type=f32)
    hidden_grad = active_back(active_grad)[0].astype(bf16)
    input_part = contract_last(hidden_grad, w_inner).astype(bf16)
    outer_grad = contract_first(grad_arrived, active_low)
    inner_grad = contract_first(arrived, hidden_grad)
    results = collect(
        jnp.concatenate([partial_rows, input_part], axis=1), experts, capacity, 2 * width
    )
    results, inner_grad, outer_grad = lax.optimization_barrier(
        (results, inner_grad, outer_grad)
    )
    inner_share, outer_share = (
        lax.psum_scatter(inner_grad[None], "dp", scatter_dimension=1, tiled=True),
        lax.psum_scatter(outer_grad[None], "dp", scatter_dimension=1, tiled=True),
    )
    tok_both = jnp.dot(place, results[0], preferred_element_type=f32) + jnp.dot(
        place, results[1], preferred_element_type=f32
    )
    expert_tok, input_tok = tok_both[:, :width], tok_both[:, width:]
    mixed = (x_mid + gate[:, None] * expert_tok).astype(bf16)
    gate_grad = jnp.sum(upstream * expert_tok, axis=1)
    logit_grad = gate_back(gate_grad)[0].astype(bf16)
    router_local = contract_first(normed_two, logit_grad)
    norm_two_grad = input_tok + contract_last(logit_grad, router_weight)
    mid_part, gain_ffn_local = norm_two_back(norm_two_grad)
    mid_grad = upstream + mid_part
    branch_grad = mid_grad.astype(bf16)
    out_block_grad = contract_first(branch_grad, attended)
    attended_grad = (
        jnp.dot(branch_grad, mixer[3 * width :], preferred_element_type=f32)
        .astype(bf16)
        .reshape(count, heads, head_dim)
    )
    prob_grad = jnp.einsum("ihd,jhd->hij", attended_grad, values, preferred_element_type=f32)
    score_grad = probs * (prob_grad - jnp.sum(prob_grad * probs, axis=-1, keepdims=True))
    bias_local = jnp.einsum("hij,ijb->bh", score_grad, bucket_hot, precision=highest)
    product_grad = (score_grad * scale).astype(bf16)
    query_grad = jnp.einsum("hij,jhd->ihd", product_grad, keys, preferred_element_type=f32).astype(
        bf16
    )
    key_grad = jnp.einsum("hij,ihd->jhd", product_grad, queries, preferred_element_type=f32).astype(
        bf16
    )
    value_grad = jnp.einsum(
        "hij,ihd->jhd", probs_low, attended_grad, preferred_element_type=f32
    ).astype(bf16)
    qkv_grad = jnp.concatenate(
        [
            query_grad.reshape(count, width),
            key_grad.reshape(count, width),
            value_grad.reshape(count, width),
        ],
        axis=1,
    )
    in_block_grad = contract_first(qkv_grad, normed_one)
    norm_one_grad = jnp.dot(qkv_grad, mixer[: 3 * width], preferred_element_type=f32)
    input_part_one, gain_attn_local = norm_one_back(norm_one_grad)
    tokens_grad = mid_grad + input_part_one
    stacked = jnp.concatenate([in_block_grad.astype(bf16), out_block_grad.astype(bf16)], axis=0)
    pieces = (bias_local, gain_attn_local, gain_ffn_local, router_local)
    flat = jnp.concatenate([piece.reshape(-1) for piece in pieces])
    flat = jnp.pad(flat, (0, -flat.shape[0] % 1024)).reshape(-1, 128)
    if cube:
        mixer_grad, total = scatter_mixer(stacked, flat)
    else:
        mixer_grad = lax.psum_scatter(
            stacked, ("dp", "expert"), scatter_dimension=0, tiled=True
        ).astype(f32)
        total = lax.psum(flat, ("dp", "expert"))
    total = total.reshape(-1)
    sums, start = [], 0
    for piece in pieces:
        sums.append(total[start : start + piece.size].reshape(piece.shape))
        start += piece.size
    bias_sum, attn_gain_sum, ffn_gain_sum, router_sum = sums
    return (
        mixed,
        tokens_grad,
        mixer_grad,
        bias_sum,
        attn_gain_sum,
        ffn_gain_sum,
        router_sum,
        inner_share,
        outer_share,
    )


def solution(mesh):
    placed = (
        P(("dp", "expert"), None),
        P(("dp", "expert"), None),
        P(("dp", "expert"), None),
        P(("dp", "expert"), None),
        P(),
        P(("dp", "expert"), None),
        P(),
        P(),
        P(),
        P(),
        P("expert", "dp", None),
        P("expert", "dp", None),
    )
    return jax.shard_map(
        shards,
        mesh=mesh,
        in_specs=placed,
        out_specs=(
            P(("dp", "expert"), None),
            P(("dp", "expert"), None),
            P(("dp", "expert"), None),
            P(),
            P(),
            P(),
            P(),
            P("expert", "dp", None),
            P("expert", "dp", None),
        ),
        check_vma=False,
    )
```

```python
import jax
import jax.numpy as jnp
from jax import lax
from jax.experimental import pallas as pl
from jax.experimental.pallas import tpu as pltpu
from jax.sharding import PartitionSpec as P


def rms_scale(rows, gain):
    inverse = lax.rsqrt(jnp.mean(rows * rows, axis=-1, keepdims=True) + 1e-06)
    return rows * inverse * gain


def gate_value(logits, chosen):
    return jnp.sum(jax.nn.softmax(logits, axis=-1) * chosen, axis=-1)


def tanh_gelu(values):
    return jax.nn.gelu(values, approximate=True)


def contract_first(left, right):
    return lax.dot_general(
        left, right, (((0,), (0,)), ((), ())), preferred_element_type=jnp.float32
    )


def contract_last(left, right):
    return lax.dot_general(
        left, right, (((1,), (1,)), ((), ())), preferred_element_type=jnp.float32
    )


def skewed_table(table, count, reach):
    offsets = jnp.arange(2 * count)
    offsets = jnp.where(offsets < count, offsets, offsets - 2 * count)
    index = jnp.clip(offsets, -reach, reach) + reach
    hot = index[:, None] == jnp.arange(table.shape[0])[None, :]
    line = jnp.sum(jnp.where(hot, table[None, :], 0), axis=1)
    flat = jnp.broadcast_to(line[None, :], (count, 2 * count)).reshape(-1)
    return flat[: count * (2 * count - 1)].reshape(count, 2 * count - 1)[:, :count]


def deliver(buffer, experts, capacity, width):
    doubled = jnp.broadcast_to(
        buffer.reshape(experts, 1, capacity, width), (experts, 2, capacity, width)
    )
    return lax.all_to_all(
        doubled.reshape(2 * experts * capacity, width),
        "expert",
        split_axis=0,
        concat_axis=0,
        tiled=True,
    )


def collect(results, experts, capacity, width):
    returned = lax.all_to_all(results, "expert", split_axis=0, concat_axis=0, tiled=True)
    returned = returned.reshape(experts, 2, capacity, width)
    return [returned[:, half].reshape(experts * capacity, width) for half in (0, 1)]


MESH = pl.DeviceIdType.MESH


def coordinates():
    core, chip = lax.axis_index("dp"), lax.axis_index("expert")
    bits = [chip // 8, (chip // 4) % 2, (chip // 2) % 2, chip % 2]
    partners = [(core, chip + (1 - 2 * bit) * step) for bit, step in zip(bits, (8, 4, 2, 1))]
    return core, bits, (1 - core, chip), partners


def meet(partners):
    barrier = pltpu.get_barrier_semaphore()
    for partner in partners:
        pl.semaphore_signal(barrier, inc=1, device_id=partner, device_id_type=MESH)
    pl.semaphore_wait(barrier, len(partners))


def gather_kernel(own_ref, out_ref, local_sem, send_sem, recv_sem):
    core, (high, low, y, x), sibling, (to_high, to_low, to_y, to_x) = coordinates()
    half = own_ref.shape[1] // 2
    left, right = pl.ds(0, half), pl.ds(half, half)
    every = slice(None)
    local = pltpu.make_async_copy(own_ref, out_ref.at[core, high, low, y, x], local_sem)
    local.start()
    meet((sibling, to_high, to_low, to_y, to_x))
    local.wait()

    def send(number, where, target):
        copy = pltpu.make_async_remote_copy(
            src_ref=out_ref.at[where],
            dst_ref=out_ref.at[where],
            send_sem=send_sem.at[number],
            recv_sem=recv_sem.at[number],
            device_id=target,
            device_id_type=MESH,
        )
        copy.start()
        return copy

    first = send(0, (core, high, low, y, x), to_high)
    first.wait_recv()
    second = send(1, (core, every, low, y, x), to_low)
    second.wait_recv()
    third_a = send(2, (core, every, every, y, x, every, left), to_y)
    third_b = send(3, (core, every, every, y, x, every, right), to_x)
    across = [send(6, (core, every, every, y, x), sibling)]
    third_a.wait_recv()
    fourth_a = send(4, (core, every, every, every, x, every, left), to_x)
    third_b.wait_recv()
    fourth_b = send(5, (core, every, every, y, every, every, right), to_y)
    across.append(send(7, (core, every, every, 1 - y, x, every, left), sibling))
    across.append(send(8, (core, every, every, y, 1 - x, every, right), sibling))
    fourth_a.wait_recv()
    across.append(send(9, (core, every, every, every, 1 - x, every, left), sibling))
    fourth_b.wait_recv()
    across.append(send(10, (core, every, every, 1 - y, every, every, right), sibling))
    for copy in across:
        copy.wait_recv()
    for copy in [first, second, third_a, third_b, fourth_a, fourth_b] + across:
        copy.wait_send()


def gather_mixer(block):
    rows, width = block.shape
    out = pl.pallas_call(
        gather_kernel,
        out_shape=jax.ShapeDtypeStruct((2, 2, 2, 2, 2, rows, width), block.dtype),
        in_specs=[pl.BlockSpec(memory_space=pl.ANY)],
        out_specs=pl.BlockSpec(memory_space=pl.ANY),
        scratch_shapes=[
            pltpu.SemaphoreType.DMA,
            pltpu.SemaphoreType.DMA((11,)),
            pltpu.SemaphoreType.DMA((11,)),
        ],
        compiler_params=pltpu.CompilerParams(collective_id=0, has_side_effects=True),
    )(block)
    return out.reshape(32 * rows, width)


def scatter_kernel(
    grad_ref,
    small_ref,
    out_ref,
    total_ref,
    whole,
    pair,
    quad,
    line,
    from_core,
    from_a,
    from_b,
    then_a,
    then_b,
    from_low,
    from_high,
    sums,
    arrived,
    send_sem,
    recv_sem,
):
    core, (high, low, y, x), sibling, (to_high, to_low, to_y, to_x) = coordinates()
    f32, bf16 = jnp.float32, jnp.bfloat16
    half = out_ref.shape[1] // 2
    left, right = pl.ds(0, half), pl.ds(half, half)
    every = slice(None)
    meet((sibling, to_high, to_low, to_y, to_x))

    def send(number, source, target_ref, target):
        copy = pltpu.make_async_remote_copy(
            src_ref=source,
            dst_ref=target_ref,
            send_sem=send_sem.at[number],
            recv_sem=recv_sem.at[number],
            device_id=target,
            device_id_type=MESH,
        )
        copy.start()
        return copy

    started = []
    order = (sibling, to_x, to_y, to_low, to_high)

    def small_start(stage):
        copy = send(7 + stage, sums.at[stage], arrived.at[stage], order[stage])
        started.append(copy)
        return copy

    def small_end(stage, copy):
        copy.wait_recv()
        sums[stage + 1] = sums[stage] + arrived[stage]

    def add(one, two):
        return one.astype(f32) + two.astype(f32)

    sums[0] = small_ref[...]
    copy = send(0, grad_ref.at[1 - core], from_core, sibling)
    small = small_start(0)
    copy.wait_recv()
    started.append(copy)
    for a in (0, 1):
        for b in (0, 1):
            for c in (0, 1):
                for d in (0, 1):
                    whole[a, b, c, d] = add(
                        grad_ref[core, a, b, c, d], from_core[a, b, c, d]
                    ).astype(bf16)
    one = send(1, whole.at[:, :, :, 1 - x, :, left], from_a, to_x)
    two = send(2, whole.at[:, :, 1 - y, :, :, right], from_b, to_y)
    started += [one, two]
    small_end(0, small)
    small = small_start(1)
    one.wait_recv()
    for a in (0, 1):
        for b in (0, 1):
            for c in (0, 1):
                pair[0, a, b, c] = add(whole[a, b, c, x, :, :half], from_a[a, b, c]).astype(bf16)
    three = send(3, pair.at[0, :, :, 1 - y], then_a, to_y)
    two.wait_recv()
    for a in (0, 1):
        for b in (0, 1):
            for c in (0, 1):
                pair[1, a, b, c] = add(whole[a, b, y, c, :, half:], from_b[a, b, c]).astype(bf16)
    four = send(4, pair.at[1, :, :, 1 - x], then_b, to_x)
    started += [three, four]
    small_end(1, small)
    small = small_start(2)
    three.wait_recv()
    four.wait_recv()
    for a in (0, 1):
        for b in (0, 1):
            quad[a, b, :, :half] = add(pair[0, a, b, y], then_a[a, b]).astype(bf16)
            quad[a, b, :, half:] = add(pair[1, a, b, x], then_b[a, b]).astype(bf16)
    five = send(5, quad.at[:, 1 - low], from_low, to_low)
    started.append(five)
    small_end(2, small)
    small = small_start(3)
    five.wait_recv()
    for a in (0, 1):
        line[a] = add(quad[a, low], from_low[a]).astype(bf16)
    six = send(6, line.at[1 - high], from_high, to_high)
    started.append(six)
    small_end(3, small)
    small = small_start(4)
    six.wait_recv()
    out_ref[...] = add(line[high], from_high[...])
    small.wait_recv()
    total_ref[...] = sums[4] + arrived[4]
    for copy in started:
        copy.wait_send()


def scatter_mixer(grad, small):
    rows, width = grad.shape[0] // 32, grad.shape[1]
    bf16, f32 = grad.dtype, jnp.float32
    half = width // 2
    vmem = pl.BlockSpec(memory_space=pltpu.VMEM)
    return pl.pallas_call(
        scatter_kernel,
        out_shape=(
            jax.ShapeDtypeStruct((rows, width), f32),
            jax.ShapeDtypeStruct(small.shape, f32),
        ),
        in_specs=[vmem, vmem],
        out_specs=(vmem, vmem),
        scratch_shapes=[
            pltpu.VMEM((2, 2, 2, 2, rows, width), bf16),
            pltpu.VMEM((2, 2, 2, 2, rows, half), bf16),
            pltpu.VMEM((2, 2, rows, width), bf16),
            pltpu.VMEM((2, rows, width), bf16),
            pltpu.VMEM((2, 2, 2, 2, rows, width), bf16),
            pltpu.VMEM((2, 2, 2, rows, half), bf16),
            pltpu.VMEM((2, 2, 2, rows, half), bf16),
            pltpu.VMEM((2, 2, rows, half), bf16),
            pltpu.VMEM((2, 2, rows, half), bf16),
            pltpu.VMEM((2, rows, width), bf16),
            pltpu.VMEM((rows, width), bf16),
            pltpu.VMEM((5,) + small.shape, f32),
            pltpu.VMEM((5,) + small.shape, f32),
            pltpu.SemaphoreType.DMA((12,)),
            pltpu.SemaphoreType.DMA((12,)),
        ],
        compiler_params=pltpu.CompilerParams(
            collective_id=1, has_side_effects=True, vmem_limit_bytes=40 * 2**20
        ),
        cost_estimate=pl.CostEstimate(
            flops=0, bytes_accessed=120 * 2**20, transcendentals=0
        ),
    )(grad.reshape(2, 2, 2, 2, 2, rows, width), small)


AWAY = (4, 3, 5, 2, 6, 1, 7)


def planes():
    core, chip = lax.axis_index("dp"), lax.axis_index("expert")
    expert, side = chip // 2, chip % 2
    peers = {step: (core, ((expert + step) % 8) * 2 + side) for step in AWAY}
    return expert, side, (core, chip + 1 - 2 * side), peers


def remote(source, target_ref, sems, number, target):
    copy = pltpu.make_async_remote_copy(
        src_ref=source,
        dst_ref=target_ref,
        send_sem=sems[0].at[number],
        recv_sem=sems[1].at[number],
        device_id=target,
        device_id_type=MESH,
    )
    copy.start()
    return copy


def dispatch_kernel(rows_ref, out_ref, local_sem, *sems):
    expert, side, twin, peers = planes()
    local = pltpu.make_async_copy(rows_ref.at[expert], out_ref.at[side, expert], local_sem)
    local.start()
    meet([twin] + [peers[step] for step in AWAY])
    out = {
        step: remote(
            rows_ref.at[(expert + step) % 8], out_ref.at[side, expert], sems, step, peers[step]
        )
        for step in AWAY
    }
    local.wait()
    across = [remote(out_ref.at[side, expert], out_ref.at[side, expert], sems, 8, twin)]
    for step in AWAY:
        out[step].wait_recv()
        origin = (expert + 8 - step) % 8
        block = out_ref.at[side, origin]
        across.append(remote(block, block, sems, 8 + step, twin))
    for copy in across:
        copy.wait_recv()
    for copy in list(out.values()) + across:
        copy.wait_send()


def collect_kernel(part_ref, out_ref, arrived, summed, *sems):
    expert, side, twin, peers = planes()
    meet([twin] + [peers[step] for step in AWAY])
    order = AWAY + (0,)
    across = {}
    for step in order:
        goal = (expert + step) % 8
        across[step] = remote(part_ref.at[1 - side, goal], arrived.at[goal], sems, step, twin)
    out = []
    for step in order:
        goal = (expert + step) % 8
        across[step].wait_recv()
        total = part_ref[side, goal].astype(jnp.float32) + arrived[goal].astype(jnp.float32)
        total = total.astype(out_ref.dtype)
        if step == 0:
            out_ref[goal] = total
        else:
            summed[goal] = total
            out.append(
                remote(summed.at[goal], out_ref.at[expert], sems, 8 + step, peers[step])
            )
    for copy in out:
        copy.wait_recv()
    for copy in out + list(across.values()):
        copy.wait_send()


def exchange(kernel, number, value, result, scratch, local):
    vmem = pl.BlockSpec(memory_space=pltpu.VMEM)
    return pl.pallas_call(
        kernel,
        out_shape=jax.ShapeDtypeStruct(result, value.dtype),
        in_specs=[vmem],
        out_specs=vmem,
        scratch_shapes=[pltpu.VMEM(result, value.dtype)] * scratch
        + [pltpu.SemaphoreType.DMA] * local
        + [pltpu.SemaphoreType.DMA((16,))] * 2,
        compiler_params=pltpu.CompilerParams(
            collective_id=number, has_side_effects=True, vmem_limit_bytes=24 * 2**20
        ),
        cost_estimate=pl.CostEstimate(flops=0, bytes_accessed=60 * 2**20, transcendentals=0),
    )(value)


def shards(
    tokens,
    cotangent,
    segment_ids,
    routes,
    bucket_table,
    mixer_weight,
    rel_bias,
    gain_attn,
    gain_ffn,
    router_weight,
    expert_in,
    expert_out,
):
    f32 = jnp.float32
    bf16 = jnp.bfloat16
    highest = lax.Precision.HIGHEST
    count, width = tokens.shape
    buckets, heads = rel_bias.shape
    head_dim = width // heads
    experts = router_weight.shape[1]
    capacity = 2 * max(1, count // experts)
    reach = (bucket_table.shape[0] - 1) // 2
    scale = head_dim ** (-0.5)
    cube = (
        lax.axis_size("dp") == 2
        and lax.axis_size("expert") == 16
        and mixer_weight.shape[0] % 16 == 0
        and width % 256 == 0
    )
    if cube:
        mixer = gather_mixer(mixer_weight)
    else:
        mixer = lax.all_gather(mixer_weight, ("dp", "expert"), axis=0, tiled=True)
    inner_all, outer_all = (
        lax.all_gather(expert_in, "dp", axis=1, tiled=True),
        lax.all_gather(expert_out, "dp", axis=1, tiled=True),
    )
    w_inner = inner_all[0]
    w_outer = outer_all[0]
    xf = tokens.astype(f32)
    norm_one, norm_one_back = jax.vjp(rms_scale, xf, gain_attn)
    normed_one = norm_one.astype(bf16)
    qkv = contract_last(normed_one, mixer[: 3 * width]).astype(bf16)
    queries = qkv[:, :width].reshape(count, heads, head_dim)
    keys = qkv[:, width : 2 * width].reshape(count, heads, head_dim)
    values = qkv[:, 2 * width :].reshape(count, heads, head_dim)
    bucket = skewed_table(bucket_table, count, reach)
    bucket_hot = (bucket[:, :, None] == jnp.arange(buckets)[None, None, :]).astype(f32)
    bias = jnp.einsum("ijb,bh->hij", bucket_hot, rel_bias, precision=highest)
    segment = segment_ids[0]
    same = (segment[:, None] == segment[None, :])[None]
    scores = jnp.einsum("ihd,jhd->hij", queries, keys, preferred_element_type=f32) * scale + bias
    scores = jnp.where(same, scores, -1e30)
    peak = jnp.max(scores, axis=-1, keepdims=True)
    weights = jnp.exp(scores - peak)
    probs = weights / jnp.sum(weights, axis=-1, keepdims=True)
    probs_low = probs.astype(bf16)
    attended = (
        jnp.einsum("hij,jhd->ihd", probs_low, values, preferred_element_type=f32)
        .astype(bf16)
        .reshape(count, width)
    )
    x_mid = xf + contract_last(attended, mixer[3 * width :])
    norm_two, norm_two_back = jax.vjp(rms_scale, x_mid, gain_ffn)
    normed_two = norm_two.astype(bf16)
    logits = jnp.dot(normed_two, router_weight, preferred_element_type=f32)
    route = routes[:, 0]
    chosen = (route[:, None] == jnp.arange(experts)[None, :]).astype(f32)
    gate, gate_back = jax.vjp(lambda scores_in: gate_value(scores_in, chosen), logits)
    below = (jnp.arange(count)[:, None] > jnp.arange(count)[None, :]).astype(bf16)
    earlier = jnp.dot(below, chosen.astype(bf16), preferred_element_type=f32)
    slot = jnp.sum(earlier * chosen, axis=1).astype(jnp.int32)
    column = route * capacity + slot
    place_hot = column[:, None] == jnp.arange(experts * capacity)[None, :]
    place = place_hot.astype(bf16)
    upstream = cotangent.astype(f32)
    expert_grad_tok = (gate[:, None] * upstream).astype(bf16)
    both = jnp.concatenate([normed_two, expert_grad_tok], axis=1)
    buffer = contract_first(place, both).astype(bf16)
    direct = cube and experts == 8 and capacity % 16 == 0
    if direct:
        arrived_both = exchange(
            dispatch_kernel,
            2,
            buffer.reshape(8, capacity, 2 * width),
            (2, 8, capacity, 2 * width),
            0,
            1,
        ).reshape(16 * capacity, 2 * width)
    else:
        arrived_both = deliver(buffer, experts, capacity, 2 * width)
    arrived, grad_arrived = arrived_both[:, :width], arrived_both[:, width:]
    hidden = jnp.dot(arrived, w_inner, preferred_element_type=f32)
    active, active_back = jax.vjp(tanh_gelu, hidden)
    active_low = active.astype(bf16)
    partial_rows = contract_last(active_low, w_outer).astype(bf16)
    active_grad = jnp.dot(grad_arrived, w_outer, preferred_element_type=f32)
    hidden_grad = active_back(active_grad)[0].astype(bf16)
    input_part = contract_last(hidden_grad, w_inner).astype(bf16)
    outer_grad = contract_first(grad_arrived, active_low)
    inner_grad = contract_first(arrived, hidden_grad)
    part = jnp.concatenate([partial_rows, input_part], axis=1)
    if direct:
        results = [
            exchange(
                collect_kernel,
                3,
                part.reshape(2, 8, capacity, 2 * width),
                (8, capacity, 2 * width),
                2,
                0,
            ).reshape(8 * capacity, 2 * width)
        ]
    else:
        results = collect(part, experts, capacity, 2 * width)
    results, inner_grad, outer_grad = lax.optimization_barrier(
        (results, inner_grad, outer_grad)
    )
    inner_share, outer_share = (
        lax.psum_scatter(inner_grad[None], "dp", scatter_dimension=1, tiled=True),
        lax.psum_scatter(outer_grad[None], "dp", scatter_dimension=1, tiled=True),
    )
    tok_both = sum(jnp.dot(place, rows, preferred_element_type=f32) for rows in results)
    expert_tok, input_tok = tok_both[:, :width], tok_both[:, width:]
    mixed = (x_mid + gate[:, None] * expert_tok).astype(bf16)
    gate_grad = jnp.sum(upstream * expert_tok, axis=1)
    logit_grad = gate_back(gate_grad)[0].astype(bf16)
    router_local = contract_first(normed_two, logit_grad)
    norm_two_grad = input_tok + contract_last(logit_grad, router_weight)
    mid_part, gain_ffn_local = norm_two_back(norm_two_grad)
    mid_grad = upstream + mid_part
    branch_grad = mid_grad.astype(bf16)
    out_block_grad = contract_first(branch_grad, attended)
    attended_grad = (
        jnp.dot(branch_grad, mixer[3 * width :], preferred_element_type=f32)
        .astype(bf16)
        .reshape(count, heads, head_dim)
    )
    prob_grad = jnp.einsum("ihd,jhd->hij", attended_grad, values, preferred_element_type=f32)
    score_grad = probs * (prob_grad - jnp.sum(prob_grad * probs, axis=-1, keepdims=True))
    bias_local = jnp.einsum("hij,ijb->bh", score_grad, bucket_hot, precision=highest)
    product_grad = (score_grad * scale).astype(bf16)
    query_grad = jnp.einsum("hij,jhd->ihd", product_grad, keys, preferred_element_type=f32).astype(
        bf16
    )
    key_grad = jnp.einsum("hij,ihd->jhd", product_grad, queries, preferred_element_type=f32).astype(
        bf16
    )
    value_grad = jnp.einsum(
        "hij,ihd->jhd", probs_low, attended_grad, preferred_element_type=f32
    ).astype(bf16)
    qkv_grad = jnp.concatenate(
        [
            query_grad.reshape(count, width),
            key_grad.reshape(count, width),
            value_grad.reshape(count, width),
        ],
        axis=1,
    )
    in_block_grad = contract_first(qkv_grad, normed_one)
    norm_one_grad = jnp.dot(qkv_grad, mixer[: 3 * width], preferred_element_type=f32)
    input_part_one, gain_attn_local = norm_one_back(norm_one_grad)
    tokens_grad = mid_grad + input_part_one
    stacked = jnp.concatenate([in_block_grad.astype(bf16), out_block_grad.astype(bf16)], axis=0)
    pieces = (bias_local, gain_attn_local, gain_ffn_local, router_local)
    flat = jnp.concatenate([piece.reshape(-1) for piece in pieces])
    flat = jnp.pad(flat, (0, -flat.shape[0] % 1024)).reshape(-1, 128)
    if cube:
        mixer_grad, total = scatter_mixer(stacked, flat)
    else:
        mixer_grad = lax.psum_scatter(
            stacked, ("dp", "expert"), scatter_dimension=0, tiled=True
        ).astype(f32)
        total = lax.psum(flat, ("dp", "expert"))
    total = total.reshape(-1)
    sums, start = [], 0
    for piece in pieces:
        sums.append(total[start : start + piece.size].reshape(piece.shape))
        start += piece.size
    bias_sum, attn_gain_sum, ffn_gain_sum, router_sum = sums
    return (
        mixed,
        tokens_grad,
        mixer_grad,
        bias_sum,
        attn_gain_sum,
        ffn_gain_sum,
        router_sum,
        inner_share,
        outer_share,
    )


def solution(mesh):
    placed = (
        P(("dp", "expert"), None),
        P(("dp", "expert"), None),
        P(("dp", "expert"), None),
        P(("dp", "expert"), None),
        P(),
        P(("dp", "expert"), None),
        P(),
        P(),
        P(),
        P(),
        P("expert", "dp", None),
        P("expert", "dp", None),
    )
    return jax.shard_map(
        shards,
        mesh=mesh,
        in_specs=placed,
        out_specs=(
            P(("dp", "expert"), None),
            P(("dp", "expert"), None),
            P(("dp", "expert"), None),
            P(),
            P(),
            P(),
            P(),
            P("expert", "dp", None),
            P("expert", "dp", None),
        ),
        check_vma=False,
    )
```
